32 devices in a mesh: halo: 2 (over x), leaf: 16 (over z, y, core).
Axes of the slice: x: 2, y: 2, z: 4, core: 2. Of those that a mesh axis runs over, the one named last changes fastest.
Arguments:
- start_modes: bfloat16 [16, 128, 8, 4, 128], P('leaf', None, 'halo'), may hold values from -6 to 6
- density: float32 [16, 8, 4, 128], P('leaf', 'halo'), may hold values from 0.5 to 4
- planes: int32 [16], P('leaf'), may hold values from 1 to 8, 75 in all
- tree_order: int32 [16], replicated, may hold values from 0 to 15, each once
- iface_index: int32 [16, 2, 128], P('leaf', None, 'halo'), may hold values from 0 to 2047
- iface_stiff: float32 [16, 2, 128], P('leaf', None, 'halo'), may hold values from 0.5 to 2
- reduced_start: float32 [384, 128], replicated, may hold values from -6 to 6
Outputs:
- modes: float32 [16, 128, 8, 4, 128], P('leaf', None, 'halo')
- reduced: float32 [16, 128, 128], P('leaf')
The draws below stay inside these ranges and needn't reach their ends.
All inputs are finite; a program needn't handle non-finite values. No bound on the sum of `planes` on one device may be relied on, other than what follows from the above.
Results may differ from the reference program's by a relative error of at most 0.0003.
Values sent between devices are 32-bit elements; how exact they have to be, the bound alone decides.
A program may use at most 64 MiB of HBM per device.

```python
import functools
import math
import jax
import jax.numpy as jnp
import numpy as np
from jax import lax

KEEP = 128
CX = 4
CY = 4
CZ = 128
ITERS = 2
RITERS = 2
LEVELS = 2
NXS = 8
CELLS = 4096
IFACE = 64
ORDER = 384
N_LEAF = 16


def place_ends(drawn, key, low, high):
    longest = drawn.shape.index(max(drawn.shape))
    spots = []
    for shift in (0, 1):
        where = [jax.random.randint(jax.random.fold_in(key, axis), (), 0, length) for axis, length in enumerate(drawn.shape)]
        where[longest] = (where[longest] + shift) % drawn.shape[longest]
        spots.append(tuple(where))
    return drawn.at[spots[0]].set(low).at[spots[1]].set(high)


def shard_levels(key, dims, split, least, largest):
    def one(axis_at, parts):
        steps = jax.random.uniform(jax.random.fold_in(jax.random.fold_in(key, 6), axis_at), (parts,), jnp.float32, least / len(split), largest / len(split))
        return jnp.repeat(jnp.exp(steps), dims[axis_at] // parts).reshape((-1,) + (1,) * (len(dims) - axis_at - 1))

    gain = one(*split[0])
    for cut in split[1:]:
        gain = gain * one(*cut)
    return gain


def profile(amount, total, reach, lean):
    portions = [(1 << 20) // math.isqrt(standing ** lean) + 1 for standing in range(2, amount + 1)]
    rest, counts = total - reach - (amount - 1), [1] * (amount - 1)
    while rest > 0:
        movable = [i for i in range(amount - 1) if counts[i] < reach]
        mass, remaining = sum([portions[i] for i in movable]), rest
        for i in movable:
            more = min(reach - counts[i], max(1, remaining * portions[i] // mass), rest)
            counts[i] = counts[i] + more
            rest = rest - more
    return np.array([reach] + counts)


def ragged_sizes(rng, amount, total, most, slope):
    if amount == 2:
        one = jax.random.randint(rng, (), max(1, total - most), min(most, total - 1) + 1)
        return jnp.stack([one, total - one])
    lengths = jnp.asarray(profile(amount, total, most, slope), jnp.int32)
    couples = (amount - 1) // 2
    source_of, taker = lengths[1:1 + 2 * couples:2], lengths[2:2 + 2 * couples:2]
    slack = jnp.minimum(source_of - 1, most - taker)
    moved = jax.random.randint(jax.random.fold_in(rng, 1), (couples,), 0, 1 << 20) % (slack + 1)
    lengths = lengths.at[1:1 + 2 * couples:2].set(source_of - moved).at[2:2 + 2 * couples:2].set(taker + moved)
    return lengths[jax.random.permutation(jax.random.fold_in(rng, 2), amount)]


def scatter_about(stream_key, shape, scale, limit, pieces=(), held_as=jnp.bfloat16):
    gain = shard_levels(stream_key, shape, pieces, -0.22, 0.18) if pieces else 1.0
    values = jax.random.normal(stream_key, shape, jnp.float32) * scale * gain
    return jnp.minimum(jnp.maximum(values, -limit), limit).astype(held_as)


def setup_inputs(seed: int = 0) -> dict:
    seeds = jax.random.split(jax.random.key(seed), 8)
    start_modes = scatter_about(seeds[0], (N_LEAF, KEEP, NXS, CY, CZ), 1.0, 6.0, ((0, 16), (2, 2)))
    density = jnp.clip(jnp.exp(math.log(4.0) - 2.0794415 * jax.random.uniform(seeds[1], (N_LEAF, NXS, CY, CZ), jnp.float32) ** shard_levels(seeds[1], (N_LEAF, NXS, CY, CZ), ((0, 16), (1, 2)), -0.2, 0.2)), 0.5, 4.0)
    planes = ragged_sizes(seeds[2], N_LEAF, (N_LEAF - 1) + NXS + (N_LEAF - 1) * (NXS - 1) // 2, NXS, 2).astype(jnp.int32)
    tree_order = jax.random.permutation(seeds[3], N_LEAF).astype(jnp.int32)
    iface_index = place_ends(jax.random.randint(seeds[4], (N_LEAF, LEVELS, KEEP), 0, CX * CY * CZ), jax.random.fold_in(seeds[4], 1), 0, (CX * CY * CZ) - 1).astype(jnp.int32)
    iface_stiff = jnp.clip(jnp.exp(math.log(2.0) - 1.3862944 * jax.random.uniform(seeds[5], (N_LEAF, LEVELS, KEEP), jnp.float32) ** shard_levels(seeds[5], (N_LEAF, LEVELS, KEEP), ((0, 16), (2, 2)), -0.2, 0.2)), 0.5, 2.0)
    reduced_start = scatter_about(seeds[6], (ORDER, KEEP), 1.0, 6.0, (), jnp.float32)
    return dict(start_modes=start_modes, density=density, planes=planes, tree_order=tree_order, iface_index=iface_index, iface_stiff=iface_stiff, reduced_start=reduced_start)


EXACT = lax.Precision.HIGHEST

def axis_smooth(values_in, axis_number):
    pads = [(1, 1) if position == axis_number else (0, 0) for position in range(values_in.ndim)]
    padded = jnp.pad(values_in, pads)
    extent = values_in.shape[axis_number]
    return 0.5 * lax.slice_in_dim(padded, 0, extent, axis=axis_number) + lax.slice_in_dim(padded, 1, extent + 1, axis=axis_number) + 0.5 * lax.slice_in_dim(padded, 2, extent + 2, axis=axis_number)

def operator_apply(vectors, density_cells, plane_mask):
    masked = vectors * plane_mask
    stacked = jnp.stack([masked, masked * density_cells])
    summed = axis_smooth(stacked, 2)
    summed = axis_smooth(summed, 3)
    summed = axis_smooth(summed, 4)
    return plane_mask * (density_cells * summed[0] + summed[1]) / 16.0

def reduce_solve(own_reduced, other_reduced, own_rows, other_rows, stiff_all, own_first, start_block, coupling_scale):
    first_reduced = jnp.where(own_first, own_reduced, other_reduced)
    second_reduced = jnp.where(own_first, other_reduced, own_reduced)
    first_rows = coupling_scale * jnp.where(own_first, own_rows, other_rows)
    second_rows = coupling_scale * jnp.where(own_first, other_rows, own_rows)
    zero_block = jnp.zeros_like(first_reduced)
    matrix = jnp.block([[first_reduced, zero_block, first_rows.T], [zero_block, second_reduced, second_rows.T], [first_rows, second_rows, jnp.diag(stiff_all)]])
    coeffs = start_block
    for inner_step in range(RITERS):
        product = jnp.dot(matrix, coeffs, precision=EXACT)
        gram_small = jnp.dot(product.T, product, precision=EXACT)
        lower_factor = jnp.linalg.cholesky(gram_small)
        coeffs = jax.scipy.linalg.solve_triangular(lower_factor, product.T, lower=True).T
    reduced_next = jnp.dot(coeffs.T, jnp.dot(matrix, coeffs, precision=EXACT), precision=EXACT)
    return (coeffs, reduced_next)

def subspace_phase(inputs):
    start_one, density_one, planes_one = inputs
    plane_mask = (jnp.arange(NXS, dtype=jnp.int32) < planes_one).astype(jnp.float32)[:, None, None]
    vectors = start_one.astype(jnp.float32)
    for iteration in range(ITERS - 1):
        vectors = operator_apply(vectors, density_one, plane_mask)
    image_rows = operator_apply(vectors, density_one, plane_mask).reshape(KEEP, CELLS)
    gram_total = jnp.einsum('kp,jp->kj', image_rows, image_rows, precision=EXACT)
    lower_factor = jnp.linalg.cholesky(gram_total)
    basis_rows = jax.scipy.linalg.solve_triangular(lower_factor, image_rows, lower=True)
    applied = operator_apply(basis_rows.reshape(KEEP, NXS, CY, CZ), density_one, plane_mask).reshape(KEEP, CELLS)
    reduced_one = jnp.einsum('kp,jp->kj', basis_rows, applied, precision=EXACT)
    return (basis_rows, reduced_one)

def reference(start_modes, density, planes, tree_order, iface_index, iface_stiff, reduced_start):
    basis_all, reduced_all = lax.map(subspace_phase, (start_modes, density, planes))
    leaf_ids = jnp.arange(N_LEAF, dtype=jnp.int32)
    coupling_scale = 0.5 * math.sqrt(CELLS / KEEP)
    for level_index in range(LEVELS):
        group_step = 2 ** level_index
        blocks = tree_order // group_step
        other_blocks = jnp.bitwise_xor(blocks, 1)
        own_mask = blocks[None, :] == blocks[:, None]
        same_mask = own_mask & (leaf_ids[None, :] != leaf_ids[:, None])
        other_mask = blocks[None, :] == other_blocks[:, None]
        rep_mask = tree_order[None, :] == (other_blocks * group_step)[:, None]
        own_least = lax.optimization_barrier(jnp.min(jnp.where(own_mask, leaf_ids[None, :], N_LEAF), axis=1))
        other_least = lax.optimization_barrier(jnp.min(jnp.where(other_mask, leaf_ids[None, :], N_LEAF), axis=1))
        own_first = own_least < other_least
        cell_index = (jnp.arange(KEEP, dtype=jnp.int32) // IFACE * (CX * CY * CZ))[None, :] + iface_index[:, level_index, :]
        rows_all = jax.vmap(lambda basis_one, index_one: jnp.take(basis_one, index_one, axis=1).T)(basis_all, cell_index)
        same_weight = same_mask.astype(jnp.float32)
        other_weight = other_mask.astype(jnp.float32)
        rep_weight = rep_mask.astype(jnp.float32)
        own_rows = rows_all + jnp.einsum('st,tjk->sjk', same_weight, rows_all, precision=EXACT)
        other_rows = jnp.einsum('st,tjk->sjk', other_weight, rows_all, precision=EXACT)
        stiffness = iface_stiff[:, level_index, :]
        stiff_all = stiffness + jnp.einsum('st,tj->sj', same_weight + other_weight, stiffness, precision=EXACT)
        other_reduced = jnp.einsum('st,tjk->sjk', rep_weight, reduced_all, precision=EXACT)
        solver = functools.partial(reduce_solve, start_block=reduced_start, coupling_scale=coupling_scale)
        coeffs_all, reduced_next = jax.vmap(solver)(reduced_all, other_reduced, own_rows, other_rows, stiff_all, own_first)
        weight_factor = 1.0 / math.sqrt(2 ** (level_index + 1))

        def update_basis(inputs):
            basis_one, coeffs_one, index_one, first_one = inputs
            own_coeffs = jnp.where(first_one, coeffs_one[:KEEP], coeffs_one[KEEP:2 * KEEP])
            iface_coeffs = coeffs_one[2 * KEEP:]
            spread = jnp.zeros((KEEP, CELLS), jnp.float32).at[:, index_one].add(weight_factor * iface_coeffs.T)
            return jnp.einsum('kj,kp->jp', own_coeffs, basis_one, precision=EXACT) + spread
        basis_all = lax.map(update_basis, (basis_all, coeffs_all, cell_index, own_first))
        reduced_all = reduced_next
    modes = (math.sqrt(CELLS) * basis_all).reshape(N_LEAF, KEEP, NXS, CY, CZ)
    return (modes, reduced_all)
```

```python
import functools
import math

import jax
import jax.numpy as jnp
from jax import lax
from jax.experimental import pallas as pl
from jax.experimental.pallas import tpu as pltpu
from jax.sharding import PartitionSpec as P

RITERS = 2
EXACT = lax.Precision.HIGHEST
VMEM_LIMIT = 48 * 1024 * 1024
F32 = jnp.float32


def nn(a, b):
    return lax.dot_general(a, b, (((1,), (0,)), ((), ())), precision=EXACT, preferred_element_type=F32)


def nt(a, b):
    return lax.dot_general(a, b, (((1,), (1,)), ((), ())), precision=EXACT, preferred_element_type=F32)


def lower_inverses(grams):
    n = grams[0].shape[0]
    wide = (8, n)
    row_ids = lax.broadcasted_iota(jnp.int32, wide, 0)
    lane_ids = lax.broadcasted_iota(jnp.int32, wide, 1)
    count = n // 8
    left = [[g[8 * i : 8 * i + 8, :] for i in range(count)] for g in grams]
    right = [[(lane_ids == row_ids + 8 * i).astype(F32) for i in range(count)] for _ in grams]

    def row_of(block, k):
        return jnp.broadcast_to(block[k : k + 1, :], wide)

    def column_of(block, k):
        return jnp.broadcast_to(block[:, k : k + 1], wide)

    for p in range(count):
        for a, b in zip(left, right):
            diag = [column_of(a[p], 8 * p + j) for j in range(8)]
            top_a, top_b = a[p], b[p]
            scales, factors, rows_a, rows_b = [], {}, [], []
            for k in range(8):
                scale = lax.rsqrt(row_of(diag[k], k))
                column = diag[k] * scale
                below = jnp.where(row_ids > k, column, 0.0)
                row_a, row_b = row_of(top_a, k) * scale, row_of(top_b, k) * scale
                top_a = top_a - below * row_a
                top_b = jnp.where(row_ids == k, row_b, top_b - below * row_b)
                for j in range(k + 1, 8):
                    factors[j, k] = row_of(column, j)
                    diag[j] = diag[j] - below * factors[j, k]
                scales.append(scale)
                rows_a.append(row_a)
                rows_b.append(row_b)
            b[p] = top_b
            for i in range(p + 1, count):
                columns = [column_of(a[i], 8 * p + j) for j in range(8)]
                new_a, new_b = a[i], b[i]
                for k in range(8):
                    c = columns[k]
                    for m in range(k):
                        c = c - columns[m] * factors[k, m]
                    columns[k] = c * scales[k]
                    new_a = new_a - columns[k] * rows_a[k]
                    new_b = new_b - columns[k] * rows_b[k]
                a[i], b[i] = new_a, new_b
    return [jnp.concatenate(b, axis=0) for b in right]


def own_kernel(sums_ref, rows_ref, inverse_ref, pack_ref):
    n = sums_ref.shape[1]
    (inverse,) = lower_inverses([sums_ref[0:n, :]])
    inverse_ref[...] = inverse
    pack_ref[0:n, :] = nt(nn(inverse, sums_ref[n : 2 * n, :]), inverse)
    pack_ref[n : 3 * n, :] = nt(rows_ref[...], inverse)


def merge_kernel(
    cells,
    local_cells,
    slot_ref,
    base_ref,
    quad_ref,
    index_row_ref,
    index_col_ref,
    stiff_ref,
    start_ref,
    inverse_ref,
    own_col_ref,
    image_ref,
    modes_ref,
    reduced_ref,
    matrix_ref,
    state_ref,
):
    n = inverse_ref.shape[0]
    coupling = 0.5 * math.sqrt(cells / n)
    eye = lax.broadcasted_iota(jnp.int32, (n, n), 0) == lax.broadcasted_iota(jnp.int32, (n, n), 1)

    def set_matrix(spot, first, second, rows_first, rows_second, stiff):
        m = matrix_ref.at[spot]
        zero = jnp.zeros((n, n), F32)
        m[0:n, 0:n] = first
        m[0:n, n : 2 * n] = zero
        m[n : 2 * n, 0:n] = zero
        m[n : 2 * n, n : 2 * n] = second
        rows_first = coupling * rows_first
        rows_second = coupling * rows_second
        m[0:n, 2 * n : 3 * n] = rows_first.T
        m[n : 2 * n, 2 * n : 3 * n] = rows_second.T
        m[2 * n : 3 * n, 0:n] = rows_first
        m[2 * n : 3 * n, n : 2 * n] = rows_second
        m[2 * n : 3 * n, 2 * n : 3 * n] = jnp.where(eye, jnp.broadcast_to(stiff, (n, n)), 0.0)

    def iterate(spots):
        for spot in spots:
            state_ref[spot] = start_ref[...]

        def step(_, carry):
            products = [nt(state_ref[s], matrix_ref[s]) for s in spots]
            inverses = lower_inverses([nt(p, p) for p in products])
            for s, p, inv in zip(spots, products, inverses):
                state_ref[s] = nn(inv, p)
            return carry

        lax.fori_loop(0, RITERS, step, 0)
        return [nt(state_ref[s], nt(state_ref[s], matrix_ref[s])) for s in spots]

    for pair in range(2):
        a, b = 2 * pair, 2 * pair + 1
        set_matrix(
            pair,
            quad_ref[a, 0:n, :],
            quad_ref[b, 0:n, :],
            quad_ref[a, n : 2 * n, :],
            quad_ref[b, n : 2 * n, :],
            stiff_ref[a, 0:1, :] + stiff_ref[b, 0:1, :],
        )
    reduced = iterate((0, 1))
    half = 1.0 / math.sqrt(2.0)
    merged = []
    for pair in range(2):
        total = None
        faces = state_ref[pair, :, 2 * n : 3 * n]
        for member in range(2):
            t = 2 * pair + member
            match = (index_col_ref[t] == index_row_ref[t]).astype(F32)
            rows = nt(quad_ref[t, 2 * n : 3 * n, :], state_ref[pair, :, member * n : member * n + n])
            rows = rows + half * nt(match, faces)
            total = rows if total is None else total + rows
        merged.append(total)
    stiff = stiff_ref[0, 1:2, :] + stiff_ref[1, 1:2, :] + stiff_ref[2, 1:2, :] + stiff_ref[3, 1:2, :]
    slot = slot_ref[0]
    in_second_pair = slot >= 2
    second_member = (slot == 1) | (slot == 3)
    zero_state = jnp.where(in_second_pair, state_ref[1], state_ref[0])
    zero_own = jnp.where(second_member, zero_state[:, n : 2 * n], zero_state[:, 0:n])
    zero_faces = zero_state[:, 2 * n : 3 * n]
    set_matrix(2, reduced[0], reduced[1], merged[0], merged[1], stiff)
    (final,) = iterate((2,))
    reduced_ref[...] = final
    one_own = jnp.where(in_second_pair, state_ref[2, :, n : 2 * n], state_ref[2, :, 0:n])
    one_faces = state_ref[2, :, 2 * n : 3 * n]
    scale = math.sqrt(cells)
    left = scale * jnp.concatenate(
        [nn(one_own, nn(zero_own, inverse_ref[...])), half * nn(one_own, zero_faces), 0.5 * one_faces], axis=1
    )
    base = base_ref[0]
    for at in range(0, local_cells, 512):
        ids = lax.broadcasted_iota(jnp.int32, (n, 512), 1) + (base + at)
        right = jnp.concatenate(
            [
                image_ref[:, at : at + 512],
                (own_col_ref[0] == ids).astype(F32),
                (own_col_ref[1] == ids).astype(F32),
            ],
            axis=0,
        )
        modes_ref[:, at : at + 512] = nn(left, right)


def vmem():
    return pl.BlockSpec(memory_space=pltpu.VMEM)


def smem():
    return pl.BlockSpec(memory_space=pltpu.SMEM)


def with_halo(cells, axis, dim, width):
    count = lax.axis_size(axis)
    ends = count - 1
    head = lax.slice_in_dim(cells, 0, width, axis=dim)
    tail = lax.slice_in_dim(cells, cells.shape[dim] - width, cells.shape[dim], axis=dim)
    return jnp.concatenate(
        [
            lax.ppermute(tail, axis, [(i, (i + 1) % count) for i in range(ends)]),
            cells,
            lax.ppermute(head, axis, [((i + 1) % count, i) for i in range(ends)]),
        ],
        axis=dim,
    )


def axis_smooth(values_in, axis_number):
    pads = [(1, 1) if position == axis_number else (0, 0) for position in range(values_in.ndim)]
    padded = jnp.pad(values_in, pads)
    extent = values_in.shape[axis_number]
    return (
        0.5 * lax.slice_in_dim(padded, 0, extent, axis=axis_number)
        + lax.slice_in_dim(padded, 1, extent + 1, axis=axis_number)
        + 0.5 * lax.slice_in_dim(padded, 2, extent + 2, axis=axis_number)
    )


def operator_apply(vectors, density_cells, plane_mask):
    masked = vectors * plane_mask
    extent = masked.shape[1]
    stacked = jnp.stack([masked, masked * density_cells])
    padded = with_halo(stacked, "halo", 2, 1)
    summed = 0.5 * padded[:, :, :extent] + padded[:, :, 1 : extent + 1] + 0.5 * padded[:, :, 2 : extent + 2]
    summed = axis_smooth(summed, 3)
    summed = axis_smooth(summed, 4)
    return plane_mask * (density_cells * summed[0] + summed[1]) / 16.0


def image_phase(start_modes, density, planes, positions):
    n = start_modes.shape[1]
    local_cells = start_modes.shape[2] * start_modes.shape[3] * start_modes.shape[4]
    halo_index = lax.axis_index("halo")
    plane_ids = halo_index * start_modes.shape[2] + jnp.arange(start_modes.shape[2], dtype=jnp.int32)
    plane_mask = (plane_ids < planes[0]).astype(F32)[:, None, None]
    vectors = start_modes[0].astype(F32)
    vectors = operator_apply(vectors, density[0], plane_mask)
    image = operator_apply(vectors, density[0], plane_mask)
    applied = operator_apply(image, density[0], plane_mask).reshape(n, local_cells)
    image = image.reshape(n, local_cells)
    both = jnp.concatenate([image, applied], axis=0)
    sums = lax.psum(jnp.einsum("jp,kp->jk", both, image, precision=EXACT), "halo")
    sums = jnp.concatenate([sums[:n], sums[n:].T], axis=0)
    rows = jnp.take(image, positions.reshape(-1), axis=1).T.reshape(2, -1, n)
    rows = lax.all_gather(rows, "halo", axis=1, tiled=True).reshape(2 * n, n)
    return image, sums, rows


def per_device(start_modes, density, planes, tree_order, iface_index, iface_stiff, reduced_start):
    n = start_modes.shape[1]
    block_shape = start_modes.shape[1:]
    local_cells = start_modes.shape[2] * start_modes.shape[3] * start_modes.shape[4]
    halo_index = lax.axis_index("halo")
    leaf_size = lax.axis_size("leaf")
    leaf_index = lax.axis_index("leaf")
    cells = local_cells * lax.axis_size("halo")
    base = halo_index * local_cells

    leaf_ids = jnp.arange(leaf_size, dtype=jnp.int32)
    pair_of = tree_order // 2
    quad_mask = tree_order // 4 == tree_order[leaf_index] // 4
    a0 = jnp.min(jnp.where(quad_mask, leaf_ids, leaf_size))
    first_pair = pair_of == tree_order[a0] // 2
    second_pair = quad_mask & ~first_pair
    b0 = jnp.max(jnp.where(first_pair, leaf_ids, -1))
    a1 = jnp.min(jnp.where(second_pair, leaf_ids, leaf_size))
    b1 = jnp.max(jnp.where(second_pair, leaf_ids, -1))
    members = jnp.stack([a0, b0, a1, b1])
    slot = jnp.sum(jnp.where(members == leaf_index, jnp.arange(4, dtype=jnp.int32), 0))

    small = jnp.concatenate([iface_stiff[0], (iface_index[0] + base).astype(F32)], axis=0)
    small = lax.all_gather(small, "halo", axis=1, tiled=True)
    small = jnp.concatenate([small, jnp.zeros_like(small)], axis=0)
    image, sums, rows = image_phase(start_modes, density, planes, iface_index[0])
    inverse, pack = pl.pallas_call(
        own_kernel,
        out_shape=(jax.ShapeDtypeStruct((n, n), F32), jax.ShapeDtypeStruct((3 * n, n), F32)),
        in_specs=[vmem()] * 2,
        out_specs=(vmem(), vmem()),
        compiler_params=pltpu.CompilerParams(vmem_limit_bytes=VMEM_LIMIT),
        name="own_problem",
    )(sums, rows)
    full = jnp.concatenate([pack, small], axis=0)
    gathered = lax.all_gather(full[None], "leaf", axis=0, tiled=True)
    quad = jnp.take(gathered, members, axis=0)
    quad_small = quad[:, 3 * n :, :]
    stiff = quad_small[:, 0:2, :]
    index_row = quad_small[:, 2:3, :]
    index_col = quad_small[:, 3, :, None]
    own_col = small[2:4, :, None].astype(jnp.int32)
    modes, reduced = pl.pallas_call(
        functools.partial(merge_kernel, cells, local_cells),
        out_shape=(jax.ShapeDtypeStruct((n, local_cells), F32), jax.ShapeDtypeStruct((n, n), F32)),
        in_specs=[smem()] * 2 + [vmem()] * 8,
        out_specs=(vmem(), vmem()),
        scratch_shapes=[pltpu.VMEM((3, 3 * n, 3 * n), F32), pltpu.VMEM((3, n, 3 * n), F32)],
        compiler_params=pltpu.CompilerParams(vmem_limit_bytes=VMEM_LIMIT),
        name="merge_problems",
    )(
        slot[None],
        base[None].astype(jnp.int32),
        quad,
        index_row,
        index_col,
        stiff,
        reduced_start.T,
        inverse,
        own_col,
        image,
    )
    return modes.reshape((1,) + tuple(block_shape)), reduced[None]


def solution(mesh):
    return jax.shard_map(
        per_device,
        mesh=mesh,
        in_specs=(
            P("leaf", None, "halo", None, None),
            P("leaf", "halo", None, None),
            P("leaf"),
            P(),
            P("leaf", None, "halo"),
            P("leaf", None, "halo"),
            P(),
        ),
        out_specs=(P("leaf", None, "halo", None, None), P("leaf", None, None)),
        check_vma=False,
    )
```

```python
import functools
import math

import jax
import jax.numpy as jnp
from jax import lax
from jax.experimental import pallas as pl
from jax.experimental.pallas import tpu as pltpu
from jax.sharding import PartitionSpec as P

RITERS = 2
EXACT = lax.Precision.HIGHEST
VMEM_LIMIT = 48 * 1024 * 1024
F32 = jnp.float32


def nn(a, b):
    return lax.dot_general(a, b, (((1,), (0,)), ((), ())), precision=EXACT, preferred_element_type=F32)


def nt(a, b):
    return lax.dot_general(a, b, (((1,), (1,)), ((), ())), precision=EXACT, preferred_element_type=F32)


def lower_inverses(grams):
    n = grams[0].shape[0]
    wide = (8, n)
    row_ids = lax.broadcasted_iota(jnp.int32, wide, 0)
    lane_ids = lax.broadcasted_iota(jnp.int32, wide, 1)
    count = n // 8
    left = [[g[8 * i : 8 * i + 8, :] for i in range(count)] for g in grams]
    right = [[(lane_ids == row_ids + 8 * i).astype(F32) for i in range(count)] for _ in grams]

    def row_of(block, k):
        return jnp.broadcast_to(block[k : k + 1, :], wide)

    def column_of(block, k):
        return jnp.broadcast_to(block[:, k : k + 1], wide)

    for p in range(count):
        for a, b in zip(left, right):
            diag = [column_of(a[p], 8 * p + j) for j in range(8)]
            top_a, top_b = a[p], b[p]
            scales, factors, rows_a, rows_b = [], {}, [], []
            for k in range(8):
                scale = lax.rsqrt(row_of(diag[k], k))
                column = diag[k] * scale
                below = jnp.where(row_ids > k, column, 0.0)
                row_a, row_b = row_of(top_a, k) * scale, row_of(top_b, k) * scale
                top_a = top_a - below * row_a
                top_b = jnp.where(row_ids == k, row_b, top_b - below * row_b)
                for j in range(k + 1, 8):
                    factors[j, k] = row_of(column, j)
                    diag[j] = diag[j] - below * factors[j, k]
                scales.append(scale)
                rows_a.append(row_a)
                rows_b.append(row_b)
            b[p] = top_b
            for i in range(p + 1, count):
                columns = [column_of(a[i], 8 * p + j) for j in range(8)]
                new_a, new_b = a[i], b[i]
                for k in range(8):
                    c = columns[k]
                    for m in range(k):
                        c = c - columns[m] * factors[k, m]
                    columns[k] = c * scales[k]
                    new_a = new_a - columns[k] * rows_a[k]
                    new_b = new_b - columns[k] * rows_b[k]
                a[i], b[i] = new_a, new_b
    return [jnp.concatenate(b, axis=0) for b in right]


def own_kernel(sums_ref, rows_ref, inverse_ref, pack_ref):
    n = sums_ref.shape[1]
    (inverse,) = lower_inverses([sums_ref[0:n, :]])
    inverse_ref[...] = inverse
    pack_ref[0:n, :] = nt(nn(inverse, sums_ref[n : 2 * n, :]), inverse)
    pack_ref[n : 3 * n, :] = nt(rows_ref[...], inverse)


def merge_kernel(
    cells,
    local_cells,
    slot_ref,
    base_ref,
    quad_ref,
    index_row_ref,
    index_col_ref,
    stiff_ref,
    start_ref,
    inverse_ref,
    own_col_ref,
    image_ref,
    modes_ref,
    reduced_ref,
    matrix_ref,
    state_ref,
):
    n = inverse_ref.shape[0]
    coupling = 0.5 * math.sqrt(cells / n)
    eye = lax.broadcasted_iota(jnp.int32, (n, n), 0) == lax.broadcasted_iota(jnp.int32, (n, n), 1)

    def set_matrix(spot, first, second, rows_first, rows_second, stiff):
        m = matrix_ref.at[spot]
        zero = jnp.zeros((n, n), F32)
        m[0:n, 0:n] = first
        m[0:n, n : 2 * n] = zero
        m[n : 2 * n, 0:n] = zero
        m[n : 2 * n, n : 2 * n] = second
        rows_first = coupling * rows_first
        rows_second = coupling * rows_second
        m[0:n, 2 * n : 3 * n] = rows_first.T
        m[n : 2 * n, 2 * n : 3 * n] = rows_second.T
        m[2 * n : 3 * n, 0:n] = rows_first
        m[2 * n : 3 * n, n : 2 * n] = rows_second
        m[2 * n : 3 * n, 2 * n : 3 * n] = jnp.where(eye, jnp.broadcast_to(stiff, (n, n)), 0.0)

    def iterate(spots):
        for spot in spots:
            state_ref[spot] = start_ref[...]

        def step(_, carry):
            products = [nt(state_ref[s], matrix_ref[s]) for s in spots]
            inverses = lower_inverses([nt(p, p) for p in products])
            for s, p, inv in zip(spots, products, inverses):
                state_ref[s] = nn(inv, p)
            return carry

        lax.fori_loop(0, RITERS, step, 0)
        return [nt(state_ref[s], nt(state_ref[s], matrix_ref[s])) for s in spots]

    for pair in range(2):
        a, b = 2 * pair, 2 * pair + 1
        set_matrix(
            pair,
            quad_ref[a, 0:n, :],
            quad_ref[b, 0:n, :],
            quad_ref[a, n : 2 * n, :],
            quad_ref[b, n : 2 * n, :],
            stiff_ref[a, 0:1, :] + stiff_ref[b, 0:1, :],
        )
    reduced = iterate((0, 1))
    half = 1.0 / math.sqrt(2.0)
    merged = []
    for pair in range(2):
        total = None
        faces = state_ref[pair, :, 2 * n : 3 * n]
        for member in range(2):
            t = 2 * pair + member
            match = (index_col_ref[t] == index_row_ref[t]).astype(F32)
            rows = nt(quad_ref[t, 2 * n : 3 * n, :], state_ref[pair, :, member * n : member * n + n])
            rows = rows + half * nt(match, faces)
            total = rows if total is None else total + rows
        merged.append(total)
    stiff = stiff_ref[0, 1:2, :] + stiff_ref[1, 1:2, :] + stiff_ref[2, 1:2, :] + stiff_ref[3, 1:2, :]
    slot = slot_ref[0]
    in_second_pair = slot >= 2
    second_member = (slot == 1) | (slot == 3)
    zero_state = jnp.where(in_second_pair, state_ref[1], state_ref[0])
    zero_own = jnp.where(second_member, zero_state[:, n : 2 * n], zero_state[:, 0:n])
    zero_faces = zero_state[:, 2 * n : 3 * n]
    set_matrix(2, reduced[0], reduced[1], merged[0], merged[1], stiff)
    (final,) = iterate((2,))
    reduced_ref[...] = final
    one_own = jnp.where(in_second_pair, state_ref[2, :, n : 2 * n], state_ref[2, :, 0:n])
    one_faces = state_ref[2, :, 2 * n : 3 * n]
    scale = math.sqrt(cells)
    left = scale * jnp.concatenate(
        [nn(one_own, nn(zero_own, inverse_ref[...])), half * nn(one_own, zero_faces), 0.5 * one_faces], axis=1
    )
    base = base_ref[0]
    for at in range(0, local_cells, 512):
        ids = lax.broadcasted_iota(jnp.int32, (n, 512), 1) + (base + at)
        right = jnp.concatenate(
            [
                image_ref[:, at : at + 512],
                (own_col_ref[0] == ids).astype(F32),
                (own_col_ref[1] == ids).astype(F32),
            ],
            axis=0,
        )
        modes_ref[:, at : at + 512] = nn(left, right)


def vmem():
    return pl.BlockSpec(memory_space=pltpu.VMEM)


def smem():
    return pl.BlockSpec(memory_space=pltpu.SMEM)


def image_kernel(
    halo_count,
    start_ref,
    density_ref,
    planes_ref,
    position_ref,
    small_ref,
    image_ref,
    sums_ref,
    rows_ref,
    small_out_ref,
    first_ref,
    applied_ref,
    from_left,
    from_right,
    density_left,
    density_right,
    parts,
    smalls,
    edge_send,
    edge_recv,
    density_send,
    density_recv,
    part_send,
    part_recv,
    small_send,
    small_recv,
):
    n = start_ref.shape[0]
    lines = density_ref.shape[0]
    extent = lines // 4
    plane = 512
    h = lax.axis_index("halo")
    has_left, has_right = h > 0, h < halo_count - 1
    left, right = lax.rem(h + halo_count - 1, halo_count), lax.rem(h + 1, halo_count)

    barrier = pltpu.get_barrier_semaphore()
    for d in range(1, halo_count):
        peer = lax.rem(h + d, halo_count)
        pl.semaphore_signal(barrier, inc=1, device_id={"halo": peer}, device_id_type=pl.DeviceIdType.MESH)
    pl.semaphore_wait(barrier, halo_count - 1)

    def send(src, dst, send_sem, recv_sem, peer):
        return pltpu.make_async_remote_copy(
            src_ref=src,
            dst_ref=dst,
            send_sem=send_sem,
            recv_sem=recv_sem,
            device_id={"halo": peer},
            device_id_type=pl.DeviceIdType.MESH,
        )

    blocks = [start_ref, first_ref, image_ref, applied_ref]
    last = (extent - 1) * plane

    def to_right(step):
        src = blocks[step].at[:, last : last + plane]
        return send(src, from_left.at[step], edge_send.at[step, 0], edge_recv.at[step, 0], right)

    def to_left(step):
        src = blocks[step].at[:, 0:plane]
        return send(src, from_right.at[step], edge_send.at[step, 1], edge_recv.at[step, 1], left)

    def density_to_right():
        return send(density_ref, density_left, density_send.at[0], density_recv.at[0], right)

    def density_to_left():
        return send(density_ref, density_right, density_send.at[1], density_recv.at[1], left)

    def start_edges(step):
        @pl.when(has_right)
        def _():
            to_right(step).start()

        @pl.when(has_left)
        def _():
            to_left(step).start()

    start_edges(0)

    @pl.when(has_right)
    def _():
        density_to_right().start()

    @pl.when(has_left)
    def _():
        density_to_left().start()

    smalls[h] = small_ref[...]

    def small_copy(d):
        peer = lax.rem(h + d, halo_count)
        return send(smalls.at[h], smalls.at[h], small_send.at[d - 1], small_recv.at[h], peer)

    for d in range(1, halo_count):
        small_copy(d).start()

    @pl.when(jnp.logical_not(has_left))
    def _():
        from_left[...] = jnp.zeros_like(from_left)
        density_left[...] = jnp.zeros_like(density_left)

    @pl.when(jnp.logical_not(has_right))
    def _():
        from_right[...] = jnp.zeros_like(from_right)
        density_right[...] = jnp.zeros_like(density_right)

    mask = [
        jnp.where(h * extent + x < planes_ref[0], jnp.float32(1.0), jnp.float32(0.0)) for x in range(-1, extent + 1)
    ]
    chunk = 32
    lane = lax.broadcasted_iota(jnp.int32, (chunk, 128), 1)

    def smooth(values):
        lower = jnp.where(lane == 0, 0.0, pltpu.roll(values, 1, 1))
        upper = jnp.where(lane == 127, 0.0, pltpu.roll(values, 127, 1))
        return 0.5 * lower + values + 0.5 * upper

    def apply_plane(step, x):
        block, out = blocks[step], blocks[step + 1]

        def body(c, carry):
            here = pl.ds(pl.multiple_of(c * chunk, chunk), chunk)
            sums_a, sums_b = [], []
            for y in range(4):
                at = y * 128
                total_a = total_b = None
                for near in (x - 1, x, x + 1):
                    if near < 0:
                        u = from_left[step, here, at : at + 128]
                        rho = density_left[lines - 4 + y : lines - 3 + y, :]
                    elif near == extent:
                        u = from_right[step, here, at : at + 128]
                        rho = density_right[y : y + 1, :]
                    else:
                        u = block[here, near * plane + at : near * plane + at + 128]
                        rho = density_ref[4 * near + y : 4 * near + y + 1, :]
                    weight = mask[near + 1] if near == x else 0.5 * mask[near + 1]
                    u = weight * u
                    v = u * rho
                    total_a = u if total_a is None else total_a + u
                    total_b = v if total_b is None else total_b + v
                sums_a.append(total_a)
                sums_b.append(total_b)
            for y in range(4):
                a, b = sums_a[y], sums_b[y]
                for other in (y - 1, y + 1):
                    if 0 <= other < 4:
                        a = a + 0.5 * sums_a[other]
                        b = b + 0.5 * sums_b[other]
                rho = density_ref[4 * x + y : 4 * x + y + 1, :]
                at = x * plane + y * 128
                out[here, at : at + 128] = (mask[x + 1] * 0.0625) * (rho * smooth(a) + smooth(b))
            return carry

        lax.fori_loop(0, n // chunk, body, 0)

    for step in range(3):
        if step > 0:
            start_edges(step)
        for x in range(1, extent - 1):
            apply_plane(step, x)

        @pl.when(has_right)
        def _():
            to_left(step).wait_recv()

        @pl.when(has_left)
        def _():
            to_right(step).wait_recv()

        if step == 0:

            @pl.when(has_right)
            def _():
                density_to_left().wait_recv()

            @pl.when(has_left)
            def _():
                density_to_right().wait_recv()

        apply_plane(step, 0)
        apply_plane(step, extent - 1)

    faces = position_ref.shape[0]
    cells = image_ref.shape[1]
    image = image_ref[...]
    ids = lax.broadcasted_iota(jnp.int32, (faces, cells), 1)
    match = (position_ref[...] == ids).astype(F32)
    parts[h, 0:n, :] = nt(image, image)
    parts[h, n : 2 * n, :] = nt(image, applied_ref[...])
    parts[h, 2 * n : 2 * n + faces, :] = nt(match, image)

    def part_copy(d):
        peer = lax.rem(h + d, halo_count)
        return send(parts.at[h], parts.at[h], part_send.at[d - 1], part_recv.at[h], peer)

    for d in range(1, halo_count):
        part_copy(d).start()
    for d in range(1, halo_count):
        peer = lax.rem(h + d, halo_count)
        send(parts.at[peer], parts.at[peer], part_send.at[d - 1], part_recv.at[peer], peer).wait_recv()
        send(smalls.at[peer], smalls.at[peer], small_send.at[d - 1], small_recv.at[peer], peer).wait_recv()
    total = parts[0, 0 : 2 * n, :]
    for j in range(1, halo_count):
        total = total + parts[j, 0 : 2 * n, :]
    sums_ref[...] = total
    half = faces // 2
    for j in range(halo_count):
        for level in range(2):
            at = level * n + j * half
            rows_ref[at : at + half, :] = parts[j, 2 * n + level * half : 2 * n + (level + 1) * half, :]
    small_out_ref[...] = smalls[...]

    for step in range(3):

        @pl.when(has_right)
        def _():
            to_right(step).wait_send()

        @pl.when(has_left)
        def _():
            to_left(step).wait_send()

    @pl.when(has_right)
    def _():
        density_to_right().wait_send()

    @pl.when(has_left)
    def _():
        density_to_left().wait_send()

    for d in range(1, halo_count):
        small_copy(d).wait_send()
        part_copy(d).wait_send()


def image_phase(start_modes, density, planes, positions, small):
    n = start_modes.shape[1]
    extent = start_modes.shape[2]
    cells = extent * start_modes.shape[3] * start_modes.shape[4]
    count = lax.axis_size("halo")
    faces = positions.size
    small = jnp.pad(small, ((0, 8 - small.shape[0]), (0, 128 - small.shape[1])))
    dma = pltpu.SemaphoreType.DMA
    image, sums, rows, smalls = pl.pallas_call(
        functools.partial(image_kernel, count),
        out_shape=(
            jax.ShapeDtypeStruct((n, cells), F32),
            jax.ShapeDtypeStruct((2 * n, n), F32),
            jax.ShapeDtypeStruct((2 * n, n), F32),
            jax.ShapeDtypeStruct((count, 8, 128), F32),
        ),
        in_specs=[vmem(), vmem(), smem(), vmem(), vmem()],
        out_specs=(vmem(),) * 4,
        scratch_shapes=[
            pltpu.VMEM((n, cells), F32),
            pltpu.VMEM((n, cells), F32),
            pltpu.VMEM((3, n, 512), F32),
            pltpu.VMEM((3, n, 512), F32),
            pltpu.VMEM((4 * extent, 128), F32),
            pltpu.VMEM((4 * extent, 128), F32),
            pltpu.VMEM((count, 2 * n + faces, n), F32),
            pltpu.VMEM((count, 8, 128), F32),
            dma((3, 2)),
            dma((3, 2)),
            dma((2,)),
            dma((2,)),
            dma((count - 1,)),
            dma((count,)),
            dma((count - 1,)),
            dma((count,)),
        ],
        compiler_params=pltpu.CompilerParams(
            collective_id=0, has_side_effects=True, vmem_limit_bytes=VMEM_LIMIT
        ),
        name="image_phase",
    )(
        start_modes[0].astype(F32).reshape(n, cells),
        density[0].reshape(4 * extent, 128),
        planes,
        positions.reshape(faces, 1),
        small,
    )
    return image, sums, rows, smalls


def per_device(start_modes, density, planes, tree_order, iface_index, iface_stiff, reduced_start):
    n = start_modes.shape[1]
    block_shape = start_modes.shape[1:]
    local_cells = start_modes.shape[2] * start_modes.shape[3] * start_modes.shape[4]
    halo_index = lax.axis_index("halo")
    leaf_size = lax.axis_size("leaf")
    leaf_index = lax.axis_index("leaf")
    cells = local_cells * lax.axis_size("halo")
    base = halo_index * local_cells

    leaf_ids = jnp.arange(leaf_size, dtype=jnp.int32)
    pair_of = tree_order // 2
    quad_mask = tree_order // 4 == tree_order[leaf_index] // 4
    a0 = jnp.min(jnp.where(quad_mask, leaf_ids, leaf_size))
    first_pair = pair_of == tree_order[a0] // 2
    second_pair = quad_mask & ~first_pair
    b0 = jnp.max(jnp.where(first_pair, leaf_ids, -1))
    a1 = jnp.min(jnp.where(second_pair, leaf_ids, leaf_size))
    b1 = jnp.max(jnp.where(second_pair, leaf_ids, -1))
    members = jnp.stack([a0, b0, a1, b1])
    slot = jnp.sum(jnp.where(members == leaf_index, jnp.arange(4, dtype=jnp.int32), 0))

    small = jnp.concatenate([iface_stiff[0], (iface_index[0] + base).astype(F32)], axis=0)
    image, sums, rows, smalls = image_phase(start_modes, density, planes, iface_index[0], small)
    small = smalls[:, :, : iface_index.shape[2]].transpose(1, 0, 2).reshape(8, n)
    inverse, pack = pl.pallas_call(
        own_kernel,
        out_shape=(jax.ShapeDtypeStruct((n, n), F32), jax.ShapeDtypeStruct((3 * n, n), F32)),
        in_specs=[vmem()] * 2,
        out_specs=(vmem(), vmem()),
        compiler_params=pltpu.CompilerParams(vmem_limit_bytes=VMEM_LIMIT),
        name="own_problem",
    )(sums, rows)
    full = jnp.concatenate([pack, small], axis=0)
    gathered = lax.all_gather(full[None], "leaf", axis=0, tiled=True)
    quad = jnp.take(gathered, members, axis=0)
    quad_small = quad[:, 3 * n :, :]
    stiff = quad_small[:, 0:2, :]
    index_row = quad_small[:, 2:3, :]
    index_col = quad_small[:, 3, :, None]
    own_col = small[2:4, :, None].astype(jnp.int32)
    modes, reduced = pl.pallas_call(
        functools.partial(merge_kernel, cells, local_cells),
        out_shape=(jax.ShapeDtypeStruct((n, local_cells), F32), jax.ShapeDtypeStruct((n, n), F32)),
        in_specs=[smem()] * 2 + [vmem()] * 8,
        out_specs=(vmem(), vmem()),
        scratch_shapes=[pltpu.VMEM((3, 3 * n, 3 * n), F32), pltpu.VMEM((3, n, 3 * n), F32)],
        compiler_params=pltpu.CompilerParams(vmem_limit_bytes=VMEM_LIMIT),
        name="merge_problems",
    )(
        slot[None],
        base[None].astype(jnp.int32),
        quad,
        index_row,
        index_col,
        stiff,
        reduced_start.T,
        inverse,
        own_col,
        image,
    )
    return modes.reshape((1,) + tuple(block_shape)), reduced[None]


def solution(mesh):
    return jax.shard_map(
        per_device,
        mesh=mesh,
        in_specs=(
            P("leaf", None, "halo", None, None),
            P("leaf", "halo", None, None),
            P("leaf"),
            P(),
            P("leaf", None, "halo"),
            P("leaf", None, "halo"),
            P(),
        ),
        out_specs=(P("leaf", None, "halo", None, None), P("leaf", None, None)),
        check_vma=False,
    )
```

```python
import functools
import math

import jax
import jax.numpy as jnp
from jax import lax
from jax.experimental import pallas as pl
from jax.experimental.pallas import tpu as pltpu
from jax.sharding import PartitionSpec as P

RITERS = 2
EXACT = lax.Precision.HIGHEST
VMEM_LIMIT = 48 * 1024 * 1024
F32 = jnp.float32


def nn(a, b):
    return lax.dot_general(a, b, (((1,), (0,)), ((), ())), precision=EXACT, preferred_element_type=F32)


def nt(a, b):
    return lax.dot_general(a, b, (((1,), (1,)), ((), ())), precision=EXACT, preferred_element_type=F32)


def lower_inverses(grams):
    n = grams[0].shape[0]
    wide = (8, n)
    row_ids = lax.broadcasted_iota(jnp.int32, wide, 0)
    lane_ids = lax.broadcasted_iota(jnp.int32, wide, 1)
    count = n // 8
    left = [[g[8 * i : 8 * i + 8, :] for i in range(count)] for g in grams]
    right = [[(lane_ids == row_ids + 8 * i).astype(F32) for i in range(count)] for _ in grams]

    def row_of(block, k):
        return jnp.broadcast_to(block[k : k + 1, :], wide)

    def column_of(block, k):
        return jnp.broadcast_to(block[:, k : k + 1], wide)

    for p in range(count):
        for a, b in zip(left, right):
            diag = [column_of(a[p], 8 * p + j) for j in range(8)]
            top_a, top_b = a[p], b[p]
            scales, factors, rows_a, rows_b = [], {}, [], []
            for k in range(8):
                scale = lax.rsqrt(row_of(diag[k], k))
                column = diag[k] * scale
                below = jnp.where(row_ids > k, column, 0.0)
                row_a, row_b = row_of(top_a, k) * scale, row_of(top_b, k) * scale
                top_a = top_a - below * row_a
                top_b = jnp.where(row_ids == k, row_b, top_b - below * row_b)
                for j in range(k + 1, 8):
                    factors[j, k] = row_of(column, j)
                    diag[j] = diag[j] - below * factors[j, k]
                scales.append(scale)
                rows_a.append(row_a)
                rows_b.append(row_b)
            b[p] = top_b
            for i in range(p + 1, count):
                columns = [column_of(a[i], 8 * p + j) for j in range(8)]
                new_a, new_b = a[i], b[i]
                for k in range(8):
                    c = columns[k]
                    for m in range(k):
                        c = c - columns[m] * factors[k, m]
                    columns[k] = c * scales[k]
                    new_a = new_a - columns[k] * rows_a[k]
                    new_b = new_b - columns[k] * rows_b[k]
                a[i], b[i] = new_a, new_b
    return [jnp.concatenate(b, axis=0) for b in right]


def own_kernel(sums_ref, rows_ref, inverse_ref, pack_ref):
    n = sums_ref.shape[1]
    (inverse,) = lower_inverses([sums_ref[0:n, :]])
    inverse_ref[...] = inverse
    pack_ref[0:n, :] = nt(nn(inverse, sums_ref[n : 2 * n, :]), inverse)
    pack_ref[n : 3 * n, :] = nt(rows_ref[...], inverse)


def merge_kernel(
    cells,
    local_cells,
    slot_ref,
    base_ref,
    quad_ref,
    index_row_ref,
    index_col_ref,
    stiff_ref,
    start_ref,
    inverse_ref,
    own_col_ref,
    image_ref,
    modes_ref,
    reduced_ref,
    matrix_ref,
    state_ref,
):
    n = inverse_ref.shape[0]
    coupling = 0.5 * math.sqrt(cells / n)
    eye = lax.broadcasted_iota(jnp.int32, (n, n), 0) == lax.broadcasted_iota(jnp.int32, (n, n), 1)

    def set_matrix(spot, first, second, rows_first, rows_second, stiff):
        m = matrix_ref.at[spot]
        zero = jnp.zeros((n, n), F32)
        m[0:n, 0:n] = first
        m[0:n, n : 2 * n] = zero
        m[n : 2 * n, 0:n] = zero
        m[n : 2 * n, n : 2 * n] = second
        rows_first = coupling * rows_first
        rows_second = coupling * rows_second
        m[0:n, 2 * n : 3 * n] = rows_first.T
        m[n : 2 * n, 2 * n : 3 * n] = rows_second.T
        m[2 * n : 3 * n, 0:n] = rows_first
        m[2 * n : 3 * n, n : 2 * n] = rows_second
        m[2 * n : 3 * n, 2 * n : 3 * n] = jnp.where(eye, jnp.broadcast_to(stiff, (n, n)), 0.0)

    def iterate(spots):
        for spot in spots:
            state_ref[spot] = start_ref[...]

        def step(_, carry):
            products = [nt(state_ref[s], matrix_ref[s]) for s in spots]
            inverses = lower_inverses([nt(p, p) for p in products])
            for s, p, inv in zip(spots, products, inverses):
                state_ref[s] = nn(inv, p)
            return carry

        lax.fori_loop(0, RITERS, step, 0)
        return [nt(state_ref[s], nt(state_ref[s], matrix_ref[s])) for s in spots]

    for pair in range(2):
        a, b = 2 * pair, 2 * pair + 1
        set_matrix(
            pair,
            quad_ref[a, 0:n, :],
            quad_ref[b, 0:n, :],
            quad_ref[a, n : 2 * n, :],
            quad_ref[b, n : 2 * n, :],
            stiff_ref[a, 0:1, :] + stiff_ref[b, 0:1, :],
        )
    reduced = iterate((0, 1))
    half = 1.0 / math.sqrt(2.0)
    merged = []
    for pair in range(2):
        total = None
        faces = state_ref[pair, :, 2 * n : 3 * n]
        for member in range(2):
            t = 2 * pair + member
            match = (index_col_ref[t] == index_row_ref[t]).astype(F32)
            rows = nt(quad_ref[t, 2 * n : 3 * n, :], state_ref[pair, :, member * n : member * n + n])
            rows = rows + half * nt(match, faces)
            total = rows if total is None else total + rows
        merged.append(total)
    stiff = stiff_ref[0, 1:2, :] + stiff_ref[1, 1:2, :] + stiff_ref[2, 1:2, :] + stiff_ref[3, 1:2, :]
    slot = slot_ref[0]
    in_second_pair = slot >= 2
    second_member = (slot == 1) | (slot == 3)
    zero_state = jnp.where(in_second_pair, state_ref[1], state_ref[0])
    zero_own = jnp.where(second_member, zero_state[:, n : 2 * n], zero_state[:, 0:n])
    zero_faces = zero_state[:, 2 * n : 3 * n]
    set_matrix(2, reduced[0], reduced[1], merged[0], merged[1], stiff)
    (final,) = iterate((2,))
    reduced_ref[...] = final
    one_own = jnp.where(in_second_pair, state_ref[2, :, n : 2 * n], state_ref[2, :, 0:n])
    one_faces = state_ref[2, :, 2 * n : 3 * n]
    scale = math.sqrt(cells)
    left = scale * jnp.concatenate(
        [nn(one_own, nn(zero_own, inverse_ref[...])), half * nn(one_own, zero_faces), 0.5 * one_faces], axis=1
    )
    base = base_ref[0]
    for at in range(0, local_cells, 512):
        ids = lax.broadcasted_iota(jnp.int32, (n, 512), 1) + (base + at)
        right = jnp.concatenate(
            [
                image_ref[:, at : at + 512],
                (own_col_ref[0] == ids).astype(F32),
                (own_col_ref[1] == ids).astype(F32),
            ],
            axis=0,
        )
        modes_ref[:, at : at + 512] = nn(left, right)


def vmem():
    return pl.BlockSpec(memory_space=pltpu.VMEM)


def smem():
    return pl.BlockSpec(memory_space=pltpu.SMEM)


def image_kernel(
    halo_count,
    start_ref,
    density_ref,
    planes_ref,
    position_ref,
    small_ref,
    image_ref,
    sums_ref,
    rows_ref,
    small_out_ref,
    first_ref,
    applied_ref,
    from_left,
    from_right,
    density_left,
    density_right,
    parts,
    smalls,
    edge_send,
    edge_recv,
    density_send,
    density_recv,
    part_send,
    part_recv,
    small_send,
    small_recv,
):
    n = start_ref.shape[0]
    lines = density_ref.shape[0]
    extent = lines // 4
    plane = 512
    h = lax.axis_index("halo")
    has_left, has_right = h > 0, h < halo_count - 1
    left, right = lax.rem(h + halo_count - 1, halo_count), lax.rem(h + 1, halo_count)

    barrier = pltpu.get_barrier_semaphore()
    for d in range(1, halo_count):
        peer = lax.rem(h + d, halo_count)
        pl.semaphore_signal(barrier, inc=1, device_id={"halo": peer}, device_id_type=pl.DeviceIdType.MESH)
    pl.semaphore_wait(barrier, halo_count - 1)

    def send(src, dst, send_sem, recv_sem, peer):
        return pltpu.make_async_remote_copy(
            src_ref=src,
            dst_ref=dst,
            send_sem=send_sem,
            recv_sem=recv_sem,
            device_id={"halo": peer},
            device_id_type=pl.DeviceIdType.MESH,
        )

    blocks = [start_ref, first_ref, image_ref, applied_ref]
    last = (extent - 1) * plane

    def to_right(step):
        src = blocks[step].at[:, last : last + plane]
        return send(src, from_left.at[step], edge_send.at[step, 0], edge_recv.at[step, 0], right)

    def to_left(step):
        src = blocks[step].at[:, 0:plane]
        return send(src, from_right.at[step], edge_send.at[step, 1], edge_recv.at[step, 1], left)

    def density_to_right():
        return send(density_ref, density_left, density_send.at[0], density_recv.at[0], right)

    def density_to_left():
        return send(density_ref, density_right, density_send.at[1], density_recv.at[1], left)

    def start_edges(step):
        @pl.when(has_right)
        def _():
            to_right(step).start()

        @pl.when(has_left)
        def _():
            to_left(step).start()

    start_edges(0)

    @pl.when(has_right)
    def _():
        density_to_right().start()

    @pl.when(has_left)
    def _():
        density_to_left().start()

    smalls[h] = small_ref[...]

    def small_copy(d):
        peer = lax.rem(h + d, halo_count)
        return send(smalls.at[h], smalls.at[h], small_send.at[d - 1], small_recv.at[h], peer)

    for d in range(1, halo_count):
        small_copy(d).start()

    @pl.when(jnp.logical_not(has_left))
    def _():
        from_left[...] = jnp.zeros_like(from_left)
        density_left[...] = jnp.zeros_like(density_left)

    @pl.when(jnp.logical_not(has_right))
    def _():
        from_right[...] = jnp.zeros_like(from_right)
        density_right[...] = jnp.zeros_like(density_right)

    mask = [
        jnp.where(h * extent + x < planes_ref[0], jnp.float32(1.0), jnp.float32(0.0)) for x in range(-1, extent + 1)
    ]
    chunk = 32
    lane = lax.broadcasted_iota(jnp.int32, (chunk, 128), 1)

    def smooth(values):
        lower = jnp.where(lane == 0, 0.0, pltpu.roll(values, 1, 1))
        upper = jnp.where(lane == 127, 0.0, pltpu.roll(values, 127, 1))
        return 0.5 * lower + values + 0.5 * upper

    def apply_plane(step, x):
        block, out = blocks[step], blocks[step + 1]

        def body(c, carry):
            here = pl.ds(pl.multiple_of(c * chunk, chunk), chunk)
            sums_a, sums_b = [], []
            for y in range(4):
                at = y * 128
                total_a = total_b = None
                for near in (x - 1, x, x + 1):
                    if near < 0:
                        u = from_left[step, here, at : at + 128]
                        rho = density_left[lines - 4 + y : lines - 3 + y, :]
                    elif near == extent:
                        u = from_right[step, here, at : at + 128]
                        rho = density_right[y : y + 1, :]
                    else:
                        u = block[here, near * plane + at : near * plane + at + 128]
                        rho = density_ref[4 * near + y : 4 * near + y + 1, :]
                    weight = mask[near + 1] if near == x else 0.5 * mask[near + 1]
                    u = weight * u
                    v = u * rho
                    total_a = u if total_a is None else total_a + u
                    total_b = v if total_b is None else total_b + v
                sums_a.append(total_a)
                sums_b.append(total_b)
            for y in range(4):
                a, b = sums_a[y], sums_b[y]
                for other in (y - 1, y + 1):
                    if 0 <= other < 4:
                        a = a + 0.5 * sums_a[other]
                        b = b + 0.5 * sums_b[other]
                rho = density_ref[4 * x + y : 4 * x + y + 1, :]
                at = x * plane + y * 128
                out[here, at : at + 128] = (mask[x + 1] * 0.0625) * (rho * smooth(a) + smooth(b))
            return carry

        lax.fori_loop(0, n // chunk, body, 0)

    for step in range(3):
        if step > 0:
            start_edges(step)
        for x in range(1, extent - 1):
            apply_plane(step, x)

        @pl.when(has_right)
        def _():
            to_left(step).wait_recv()

        @pl.when(has_left)
        def _():
            to_right(step).wait_recv()

        if step == 0:

            @pl.when(has_right)
            def _():
                density_to_left().wait_recv()

            @pl.when(has_left)
            def _():
                density_to_right().wait_recv()

        apply_plane(step, 0)
        apply_plane(step, extent - 1)

    faces = position_ref.shape[0]
    cells = image_ref.shape[1]
    image = image_ref[...]
    ids = lax.broadcasted_iota(jnp.int32, (faces, cells), 1)
    match = (position_ref[...] == ids).astype(F32)
    parts[h, 0:n, :] = nt(image, image)
    parts[h, n : 2 * n, :] = nt(image, applied_ref[...])
    parts[h, 2 * n : 2 * n + faces, :] = nt(match, image)

    def part_copy(d):
        peer = lax.rem(h + d, halo_count)
        return send(parts.at[h], parts.at[h], part_send.at[d - 1], part_recv.at[h], peer)

    for d in range(1, halo_count):
        part_copy(d).start()
    for d in range(1, halo_count):
        peer = lax.rem(h + d, halo_count)
        send(parts.at[peer], parts.at[peer], part_send.at[d - 1], part_recv.at[peer], peer).wait_recv()
        send(smalls.at[peer], smalls.at[peer], small_send.at[d - 1], small_recv.at[peer], peer).wait_recv()
    total = parts[0, 0 : 2 * n, :]
    for j in range(1, halo_count):
        total = total + parts[j, 0 : 2 * n, :]
    sums_ref[...] = total
    half = faces // 2
    for j in range(halo_count):
        for level in range(2):
            at = level * n + j * half
            rows_ref[at : at + half, :] = parts[j, 2 * n + level * half : 2 * n + (level + 1) * half, :]
    small_out_ref[...] = smalls[...]

    for step in range(3):

        @pl.when(has_right)
        def _():
            to_right(step).wait_send()

        @pl.when(has_left)
        def _():
            to_left(step).wait_send()

    @pl.when(has_right)
    def _():
        density_to_right().wait_send()

    @pl.when(has_left)
    def _():
        density_to_left().wait_send()

    for d in range(1, halo_count):
        small_copy(d).wait_send()
        part_copy(d).wait_send()


def image_phase(start_modes, density, planes, positions, small):
    n = start_modes.shape[1]
    extent = start_modes.shape[2]
    cells = extent * start_modes.shape[3] * start_modes.shape[4]
    count = lax.axis_size("halo")
    faces = positions.size
    small = jnp.pad(small, ((0, 8 - small.shape[0]), (0, 128 - small.shape[1])))
    dma = pltpu.SemaphoreType.DMA
    image, sums, rows, smalls = pl.pallas_call(
        functools.partial(image_kernel, count),
        out_shape=(
            jax.ShapeDtypeStruct((n, cells), F32),
            jax.ShapeDtypeStruct((2 * n, n), F32),
            jax.ShapeDtypeStruct((2 * n, n), F32),
            jax.ShapeDtypeStruct((count, 8, 128), F32),
        ),
        in_specs=[vmem(), vmem(), smem(), vmem(), vmem()],
        out_specs=(vmem(),) * 4,
        scratch_shapes=[
            pltpu.VMEM((n, cells), F32),
            pltpu.VMEM((n, cells), F32),
            pltpu.VMEM((3, n, 512), F32),
            pltpu.VMEM((3, n, 512), F32),
            pltpu.VMEM((4 * extent, 128), F32),
            pltpu.VMEM((4 * extent, 128), F32),
            pltpu.VMEM((count, 2 * n + faces, n), F32),
            pltpu.VMEM((count, 8, 128), F32),
            dma((3, 2)),
            dma((3, 2)),
            dma((2,)),
            dma((2,)),
            dma((count - 1,)),
            dma((count,)),
            dma((count - 1,)),
            dma((count,)),
        ],
        compiler_params=pltpu.CompilerParams(
            collective_id=0, has_side_effects=True, vmem_limit_bytes=VMEM_LIMIT
        ),
        name="image_phase",
    )(
        start_modes[0].astype(F32).reshape(n, cells),
        density[0].reshape(4 * extent, 128),
        planes,
        positions.reshape(faces, 1),
        small,
    )
    return image, sums, rows, smalls


def per_device(start_modes, density, planes, tree_order, iface_index, iface_stiff, reduced_start):
    n = start_modes.shape[1]
    block_shape = start_modes.shape[1:]
    local_cells = start_modes.shape[2] * start_modes.shape[3] * start_modes.shape[4]
    halo_index = lax.axis_index("halo")
    leaf_size = lax.axis_size("leaf")
    leaf_index = lax.axis_index("leaf")
    cells = local_cells * lax.axis_size("halo")
    base = halo_index * local_cells

    leaf_ids = jnp.arange(leaf_size, dtype=jnp.int32)
    pair_of = tree_order // 2
    quad_mask = tree_order // 4 == tree_order[leaf_index] // 4
    a0 = jnp.min(jnp.where(quad_mask, leaf_ids, leaf_size))
    first_pair = pair_of == tree_order[a0] // 2
    second_pair = quad_mask & ~first_pair
    b0 = jnp.max(jnp.where(first_pair, leaf_ids, -1))
    a1 = jnp.min(jnp.where(second_pair, leaf_ids, leaf_size))
    b1 = jnp.max(jnp.where(second_pair, leaf_ids, -1))
    members = jnp.stack([a0, b0, a1, b1])
    slot = jnp.sum(jnp.where(members == leaf_index, jnp.arange(4, dtype=jnp.int32), 0))

    small = jnp.concatenate([iface_stiff[0], (iface_index[0] + base).astype(F32)], axis=0)
    image, sums, rows, smalls = image_phase(start_modes, density, planes, iface_index[0], small)
    small = smalls[:, :, : iface_index.shape[2]].transpose(1, 0, 2).reshape(8, n)
    inverse, pack = pl.pallas_call(
        own_kernel,
        out_shape=(jax.ShapeDtypeStruct((n, n), F32), jax.ShapeDtypeStruct((3 * n, n), F32)),
        in_specs=[vmem()] * 2,
        out_specs=(vmem(), vmem()),
        compiler_params=pltpu.CompilerParams(vmem_limit_bytes=VMEM_LIMIT),
        name="own_problem",
    )(sums, rows)
    full = jnp.concatenate([pack, small], axis=0)
    halo_size = lax.axis_size("halo")
    share = -(-full.shape[0] // (8 * halo_size)) * 8
    full = jnp.pad(full, ((0, share * halo_size - full.shape[0]), (0, 0)))
    piece = lax.dynamic_slice_in_dim(full, halo_index * share, share, 0)
    gathered = lax.all_gather(piece[None], "leaf", axis=0, tiled=True)
    quad = lax.all_gather(jnp.take(gathered, members, axis=0), "halo", axis=1, tiled=True)
    quad_small = quad[:, 3 * n :, :]
    stiff = quad_small[:, 0:2, :]
    index_row = quad_small[:, 2:3, :]
    index_col = quad_small[:, 3, :, None]
    own_col = small[2:4, :, None].astype(jnp.int32)
    modes, reduced = pl.pallas_call(
        functools.partial(merge_kernel, cells, local_cells),
        out_shape=(jax.ShapeDtypeStruct((n, local_cells), F32), jax.ShapeDtypeStruct((n, n), F32)),
        in_specs=[smem()] * 2 + [vmem()] * 8,
        out_specs=(vmem(), vmem()),
        scratch_shapes=[pltpu.VMEM((3, 3 * n, 3 * n), F32), pltpu.VMEM((3, n, 3 * n), F32)],
        compiler_params=pltpu.CompilerParams(vmem_limit_bytes=VMEM_LIMIT),
        name="merge_problems",
    )(
        slot[None],
        base[None].astype(jnp.int32),
        quad,
        index_row,
        index_col,
        stiff,
        reduced_start.T,
        inverse,
        own_col,
        image,
    )
    return modes.reshape((1,) + tuple(block_shape)), reduced[None]


def solution(mesh):
    return jax.shard_map(
        per_device,
        mesh=mesh,
        in_specs=(
            P("leaf", None, "halo", None, None),
            P("leaf", "halo", None, None),
            P("leaf"),
            P(),
            P("leaf", None, "halo"),
            P("leaf", None, "halo"),
            P(),
        ),
        out_specs=(P("leaf", None, "halo", None, None), P("leaf", None, None)),
        check_vma=False,
    )
```
